256 devices in a mesh: seq: 64 (over y_lo, z, x), pipe: 4 (over y_hi, core).
Axes of the slice: x: 4, y: 4 (y_hi: 2, y_lo: 2; y = y_hi * 2 + y_lo), z: 8, core: 2. Of those that a mesh axis runs over, the one named last changes fastest.
Arguments:
- noisy_q: bfloat16 [4, 4096, 8192], P('pipe', 'seq'), may hold values from -8 to 8
- noisy_k: bfloat16 [4, 4096, 1024], P('pipe', 'seq'), may hold values from -8 to 8
- noisy_v: bfloat16 [4, 4096, 1024], P('pipe', 'seq'), may hold values from -6 to 6
- clean_k: bfloat16 [4, 4096, 1024], P('pipe', 'seq'), may hold values from -6 to 6
- clean_v: bfloat16 [4, 4096, 1024], P('pipe', 'seq'), may hold values from -6 to 6
- noisy_o: bfloat16 [4, 4096, 8192], P('pipe', 'seq'), may hold values from -6 to 6
- out_grad: bfloat16 [4, 4096, 8192], P('pipe', 'seq'), may hold values from -6 to 6
- block_mask: int32 [4, 32, 32], P('pipe'), may hold values 0 or 1
Outputs:
- passed_grad: bfloat16 [4, 4096, 8192], P('pipe', 'seq')
- noisy_k_grad: bfloat16 [4, 4096, 1024], P('pipe', 'seq')
- noisy_v_grad: bfloat16 [4, 4096, 1024], P('pipe', 'seq')
- clean_k_grad: bfloat16 [4, 4096, 1024], P('pipe', 'seq')
- clean_v_grad: bfloat16 [4, 4096, 1024], P('pipe', 'seq')
The draws below stay inside these ranges and needn't reach their ends.
All inputs are finite; a program needn't handle non-finite values. No bound on the sum of `block_mask` on one device may be relied on, other than what follows from the above.
Results may differ from the reference program's by a relative error of at most 0.0058.
Values may be sent and summed in bfloat16 or wider, within the bound.
A program may use at most 128 MiB of HBM per device.

```python
import jax
import jax.numpy as jnp
from jax import lax

HEADS = 64
KV_HEADS = 8
HEAD_FEATURES = 128
BLOCK = 128
WINDOW = 4
SECTIONS = 4
NOISY_TOKENS = 4096
BLOCKS = 32


def draw_noisy_q(key, part):
    key = jax.random.fold_in(key, 5)
    shape = (SECTIONS, BLOCKS, BLOCK, HEADS, HEAD_FEATURES)
    base = jax.random.truncated_normal(key, -6.0, 6.0, shape, jnp.float32)
    return base.reshape(SECTIONS, NOISY_TOKENS, HEADS * HEAD_FEATURES).astype(jnp.bfloat16)


def draw_noisy_k(key, part):
    key = jax.random.fold_in(key, 9)
    shape = (SECTIONS, BLOCKS, BLOCK, KV_HEADS, HEAD_FEATURES)
    base = jax.random.truncated_normal(key, -6.0, 6.0, shape, jnp.float32)
    return base.reshape(SECTIONS, NOISY_TOKENS, KV_HEADS * HEAD_FEATURES).astype(jnp.bfloat16)


def touch_ends(array, rng, least, high):
    place = [jax.random.randint(jax.random.fold_in(rng, axis), (), 0, length) for axis, length in enumerate(array.shape)]
    widest = array.shape.index(max(array.shape))
    neighbour = place[:widest] + [(place[widest] + 1) % array.shape[widest]] + place[widest + 1:]
    return array.at[tuple(place)].set(least).at[tuple(neighbour)].set(high)


def steps_of(rng, shape, cuts, low, high):
    loudness = 1.0
    for axis_at, shards_of in cuts:
        draws = jax.random.uniform(jax.random.fold_in(jax.random.fold_in(rng, 6), axis_at), (shards_of,), jnp.float32, low / len(cuts), high / len(cuts))
        loudness = loudness * jnp.repeat(jnp.exp(draws), shape[axis_at] // shards_of).reshape((-1,) + (1,) * (len(shape) - 1 - axis_at))
    return loudness


def bell_draw(key, extent, width, limit, cuts=(), kind=jnp.bfloat16):
    entries = width * jax.random.normal(key, extent, jnp.float32)
    if cuts:
        entries = entries * steps_of(key, extent, cuts, -0.22, 0.18)
    return jnp.clip(entries, -limit, limit).astype(kind)


def setup_inputs(seed: int = 0) -> dict:
    key_list = jax.random.split(jax.random.key(seed), 9)
    return {
        "noisy_q": draw_noisy_q(jax.random.fold_in(key_list[8], 71), 0),
        "noisy_k": draw_noisy_k(jax.random.fold_in(key_list[8], 71), 0),
        "noisy_v": bell_draw(key_list[2], (SECTIONS, NOISY_TOKENS, KV_HEADS * HEAD_FEATURES), 1.0, 6.0, ((0, 4), (1, 64))),
        "clean_k": bell_draw(key_list[3], (SECTIONS, NOISY_TOKENS, KV_HEADS * HEAD_FEATURES), 1.0, 6.0, ((0, 4), (1, 64))),
        "clean_v": bell_draw(key_list[4], (SECTIONS, NOISY_TOKENS, KV_HEADS * HEAD_FEATURES), 1.0, 6.0, ((0, 4), (1, 64))),
        "noisy_o": bell_draw(key_list[5], (SECTIONS, NOISY_TOKENS, HEADS * HEAD_FEATURES), 1.0, 6.0, ((0, 4), (1, 64))),
        "out_grad": bell_draw(key_list[6], (SECTIONS, NOISY_TOKENS, HEADS * HEAD_FEATURES), 1.0, 6.0, ((0, 4), (1, 64))),
        "block_mask": touch_ends((jax.random.randint(key_list[7], (SECTIONS, BLOCKS, BLOCKS), 0, 2) < 1).astype(jnp.int32), jax.random.fold_in(key_list[7], 1), 0, 1),
    }


def head_grads(queries, key_n, value_n, key_c, value_c, saved_out, grad_out, visible):
    logit_scale = HEAD_FEATURES ** -0.5
    query_block_rows = queries.astype(jnp.float32).reshape(BLOCKS, BLOCK, HEAD_FEATURES)
    key_block_rows = key_n.astype(jnp.float32).reshape(BLOCKS, BLOCK, HEAD_FEATURES)
    value_block_rows = value_n.astype(jnp.float32).reshape(BLOCKS, BLOCK, HEAD_FEATURES)
    gradient_block_rows = grad_out.astype(jnp.float32).reshape(BLOCKS, BLOCK, HEAD_FEATURES)
    noisy_scores = logit_scale * jnp.einsum('jim,jfm->jif', query_block_rows, key_block_rows)
    scores_c = logit_scale * jnp.dot(queries, key_c.T, preferred_element_type=jnp.float32)
    scores_c = jnp.where(visible, scores_c, jnp.float32(-1e30))
    row_top = jnp.maximum(noisy_scores.max(-1).reshape(NOISY_TOKENS), scores_c.max(-1))
    row_total = jnp.exp(noisy_scores - row_top.reshape(BLOCKS, BLOCK, 1)).sum(-1).reshape(NOISY_TOKENS)
    row_total = row_total + jnp.exp(scores_c - row_top[:, None]).sum(-1)
    row_lse = row_top + jnp.log(row_total)
    probs_n = jnp.exp(noisy_scores - row_lse.reshape(BLOCKS, BLOCK, 1))
    probs_c = jnp.exp(scores_c - row_lse[:, None])
    row_delta = jnp.sum(grad_out.astype(jnp.float32) * saved_out.astype(jnp.float32), -1)
    noisy_prob_gradient = jnp.einsum('jim,jfm->jif', gradient_block_rows, value_block_rows)
    dprob_c = jnp.dot(grad_out, value_c.T, preferred_element_type=jnp.float32)
    noisy_score_gradient = (probs_n * (noisy_prob_gradient - row_delta.reshape(BLOCKS, BLOCK, 1))).astype(jnp.bfloat16)
    dscore_c = (probs_c * (dprob_c - row_delta[:, None])).astype(jnp.bfloat16)
    query_gradient = jnp.einsum('fuy,fys->fus', noisy_score_gradient.astype(jnp.float32), key_block_rows).reshape(NOISY_TOKENS, HEAD_FEATURES)
    query_gradient = query_gradient + jnp.dot(dscore_c, key_c, preferred_element_type=jnp.float32)
    query_gradient = (logit_scale * query_gradient).astype(jnp.bfloat16)
    noisy_key_gradient = logit_scale * jnp.einsum('aeh,aep->ahp', noisy_score_gradient.astype(jnp.float32), query_block_rows)
    noisy_key_gradient = noisy_key_gradient.reshape(NOISY_TOKENS, HEAD_FEATURES).astype(jnp.bfloat16)
    noisy_block_probs = probs_n.astype(jnp.bfloat16).astype(jnp.float32)
    noisy_value_gradient = jnp.einsum('aeh,aep->ahp', noisy_block_probs, gradient_block_rows).reshape(NOISY_TOKENS, HEAD_FEATURES).astype(jnp.bfloat16)
    dkey_c = (logit_scale * jnp.dot(dscore_c.T, queries, preferred_element_type=jnp.float32)).astype(jnp.bfloat16)
    dvalue_c = jnp.dot(probs_c.astype(jnp.bfloat16).T, grad_out, preferred_element_type=jnp.float32).astype(jnp.bfloat16)
    return query_gradient, noisy_key_gradient, noisy_value_gradient, dkey_c, dvalue_c


def fold_groups(per_head):
    group_size = HEADS // KV_HEADS
    summed = per_head.astype(jnp.float32).reshape(KV_HEADS, group_size, NOISY_TOKENS, HEAD_FEATURES).sum(1)
    return summed.astype(jnp.bfloat16).transpose(1, 0, 2).reshape(NOISY_TOKENS, KV_HEADS * HEAD_FEATURES)


def reference(noisy_q, noisy_k, noisy_v, clean_k, clean_v, noisy_o, out_grad, block_mask):
    group_size = HEADS // KV_HEADS
    query_grads = []
    kn_list, vn_list, kc_list, vc_list = [], [], [], []
    for section in range(SECTIONS):
        by_head = lambda arr, count: arr[section].reshape(NOISY_TOKENS, count, HEAD_FEATURES).transpose(1, 0, 2)
        queries_all = by_head(noisy_q, HEADS)
        saved_all = by_head(noisy_o, HEADS)
        grads_all = by_head(out_grad, HEADS)
        keys_n = by_head(noisy_k, KV_HEADS)
        values_n = by_head(noisy_v, KV_HEADS)
        keys_c = by_head(clean_k, KV_HEADS)
        values_c = by_head(clean_v, KV_HEADS)
        block_ids = jnp.arange(BLOCKS, dtype=jnp.int32)
        allowed = ((block_mask[section] == 1) & (block_ids[None, :] < block_ids[:, None])
                   & (block_ids[None, :] >= block_ids[:, None] - WINDOW))
        visible = jnp.repeat(jnp.repeat(allowed, BLOCK, axis=0), BLOCK, axis=1)

        def per_head(inputs):
            queries, saved_out, grad_out, head_index = inputs
            kv_index = (head_index // group_size).astype(jnp.int32)
            pick = lambda arr: lax.dynamic_index_in_dim(arr, kv_index, 0, keepdims=False)
            return head_grads(queries, pick(keys_n), pick(values_n), pick(keys_c), pick(values_c),
                              saved_out, grad_out, visible)

        query_gradient, noisy_key_gradient, noisy_value_gradient, dkey_c, dvalue_c = lax.map(
            per_head, (queries_all, saved_all, grads_all, jnp.arange(HEADS, dtype=jnp.int32)))
        query_grads.append(query_gradient.transpose(1, 0, 2).reshape(NOISY_TOKENS, HEADS * HEAD_FEATURES))
        kn_list.append(fold_groups(noisy_key_gradient))
        vn_list.append(fold_groups(noisy_value_gradient))
        kc_list.append(fold_groups(dkey_c))
        vc_list.append(fold_groups(dvalue_c))
    passed_grad = jnp.stack([query_grads[(section + 1) % SECTIONS] for section in range(SECTIONS)])
    return (passed_grad, jnp.stack(kn_list), jnp.stack(vn_list), jnp.stack(kc_list), jnp.stack(vc_list))
```

```python
import functools
import math

import jax
import jax.numpy as jnp
from jax import lax
from jax.experimental import pallas as pl
from jax.experimental.pallas import tpu as pltpu
from jax.sharding import PartitionSpec as P

F = 128
GROUP = 8
CHUNKS = 8
LEVELS = 16
BLOCKS = 32
TOK = 64
ROWS = GROUP * TOK
SCALE = 1.0 / math.sqrt(F)
LOG2E = 1.4426950408889634
MESH = pl.DeviceIdType.MESH
BF = jnp.bfloat16
F32 = jnp.float32

N, Z1, Z2, Z4, B2, S1, S3, QO, PO = range(9)


def dot(a, b, ca, cb):
    return lax.dot_general(a, b, (((ca,), (cb,)), ((), ())), preferred_element_type=F32)


def body(
    q_in, kn_in, vn_in, kc_in, vc_in, o_in, g_in, mask,
    pg_out, nk_out, nv_out, ck_out, cv_out,
    qs, gs, os, win, noisy, part, own_n, land, dqs,
    big_sem, kv_sem, in_send, in_recv, out_send, out_recv, dq_send, dq_recv,
):
    seq = lax.axis_index("seq")
    pipe = lax.axis_index("pipe")
    lev = seq // 4
    x = seq % 4
    r = x // 2
    par = x % 2
    other = 1 - par
    blk = 2 * lev + r

    mate = (lev * 4 + r * 2 + other, pipe)
    inter = (lev * 4 + 3 - x, pipe)

    def level(step):
        return (((lev + step + LEVELS) % LEVELS) * 4 + x, pipe)

    up1, up2, down1, down2 = level(1), level(2), level(-1), level(-2)
    pipe_to = (seq, (pipe + 3) % 4)
    pipe_from = (seq, (pipe + 1) % 4)

    barrier = pltpu.get_barrier_semaphore()
    for device in (mate, inter, up1, up2, down1, down2, pipe_to, pipe_from):
        pl.semaphore_signal(barrier, inc=1, device_id=device, device_id_type=MESH)

    def kv_load(c, i):
        src = (kc_in, vc_in, kn_in, vn_in)[i]
        dst = (win.at[c, 8, 0], win.at[c, 8, 1], noisy.at[c, 0, 0], noisy.at[c, 0, 1])[i]
        cols = pl.ds(pl.multiple_of(c * F, F), F)
        return pltpu.make_async_copy(src.at[0, :, cols], dst, kv_sem.at[c, i])

    def big_load(c, i):
        src = (q_in, g_in, o_in)[i]
        dst = (qs, gs, os)[i].at[c]
        cols = pl.ds(pl.multiple_of(c * GROUP * F, F), GROUP * F)
        return pltpu.make_async_copy(src.at[0, :, cols], dst, big_sem.at[c, i])

    def load_kv(c, _):
        for i in range(4):
            kv_load(c, i).start()
        return 0

    def load_big(c, _):
        for i in range(3):
            big_load(c, i).start()
        return 0

    lax.fori_loop(0, CHUNKS, load_kv, 0)
    lax.fori_loop(0, CHUNKS, load_big, 0)

    zero = jnp.zeros((2, TOK, F), BF)

    def clear(pred, ref, slots):
        @pl.when(pred)
        def _():
            def one(c, _):
                for s in slots:
                    ref[c, s] = zero
                return 0

            lax.fori_loop(0, CHUNKS, one, 0)

    clear(lev < 1, win, (2 + par, 6 + other))
    clear(lev < 2, win, (6 + par,))
    clear(lev > LEVELS - 2, land, (Z1, Z4))
    clear(lev > LEVELS - 3, land, (Z2,))

    def send_in(m, c, src, dst, device):
        return pltpu.make_async_remote_copy(
            src_ref=src, dst_ref=dst, send_sem=in_send.at[m, c], recv_sem=in_recv.at[m, c],
            device_id=device, device_id_type=MESH,
        )

    def slot(c, d, p):
        return win.at[c, 2 * d + p]

    def msg_in(m, c):
        if m == N:
            return send_in(m, c, noisy.at[c, 0], noisy.at[c, 1], mate)
        if m == Z1:
            return send_in(m, c, win.at[c, 8], slot(c, 1, par), up1)
        if m == Z2:
            return send_in(m, c, win.at[c, 8], slot(c, 3, par), up2)
        if m == Z4:
            return send_in(m, c, slot(c, 1, other), slot(c, 3, other), up1)
        if m == B2:
            return send_in(m, c, slot(c, 1, par), slot(c, 1, par), mate)
        if m == S1:
            return send_in(m, c, win.at[c, 8 - r * (6 - par)], slot(c, 0, par), inter)
        if m == S3:
            return send_in(m, c, slot(c, 1 + 2 * r, par), slot(c, 2, par), inter)
        if m == QO:
            return send_in(m, c, slot(c, 1, other), slot(c, 2 - 2 * r, other), inter)
        return send_in(m, c, slot(c, 2 - 2 * r, other), slot(c, 2 - 2 * r, other), mate)

    def msg_out(m, c):
        src = {
            N: part.at[c, 8],
            PO: part.at[c, 2 * (2 - 2 * r) + par],
            QO: part.at[c, 2 * (2 * r) + par],
            Z4: part.at[c, 6 + other],
            B2: part.at[c, 2 + other],
            S1: part.at[c, 0 + other],
            S3: part.at[c, 4 + other],
            Z1: part.at[c, 2 + par],
            Z2: part.at[c, 6 + par],
        }[m]
        device = {
            N: mate, PO: mate, B2: mate, QO: inter, S1: inter, S3: inter,
            Z4: down1, Z1: down1, Z2: down2,
        }[m]
        return pltpu.make_async_remote_copy(
            src_ref=src, dst_ref=land.at[c, m], send_sem=out_send.at[m, c], recv_sem=out_recv.at[m, c],
            device_id=device, device_id_type=MESH,
        )

    def dq_copy(c):
        cols = pl.ds(pl.multiple_of(c * GROUP * F, F), GROUP * F)
        return pltpu.make_async_remote_copy(
            src_ref=dqs.at[c], dst_ref=pg_out.at[0, :, cols], send_sem=dq_send.at[c], recv_sem=dq_recv.at[c],
            device_id=pipe_to, device_id_type=MESH,
        )

    SENDS_IN = {Z1: lev < LEVELS - 1, Z2: lev < LEVELS - 2, Z4: lev < LEVELS - 1}
    GETS_IN = {Z1: lev > 0, Z2: lev > 1, Z4: lev > 0}
    SENDS_OUT, GETS_OUT = GETS_IN, SENDS_IN

    def guarded(table, m, act):
        if m in table:
            pl.when(table[m])(act)
        else:
            act()

    def start_in(m, c):
        guarded(SENDS_IN, m, lambda: msg_in(m, c).start())

    def wait_in(m, c):
        guarded(GETS_IN, m, lambda: msg_in(m, c).wait_recv())

    def start_out(m, c):
        guarded(SENDS_OUT, m, lambda: msg_out(m, c).start())

    def wait_out(m, c):
        guarded(GETS_OUT, m, lambda: msg_out(m, c).wait_recv())

    def first_hop(c):
        for i in range(4):
            kv_load(c, i).wait()
        start_in(Z1, c)
        start_in(N, c)

        @pl.when(r == 0)
        def _():
            start_in(S1, c)

        start_in(Z2, c)

    def second_hop(c):
        wait_in(Z1, c)
        start_in(B2, c)

        @pl.when(r == 1)
        def _():
            start_in(S1, c)

        wait_in(Z2, c)
        start_in(S3, c)

    def third_hop(c):
        wait_in(B2, c)
        start_in(QO, c)
        start_in(Z4, c)
        wait_in(S1, c)
        wait_in(S3, c)
        start_in(PO, c)

    bias = []
    for d in range(4):
        flag = mask[0, blk, (blk + BLOCKS - 1 - d) % BLOCKS]
        bias.append(jnp.where((blk - 1 - d >= 0) & (flag == 1), jnp.float32(0.0), jnp.float32(-1e30)))

    def compute(c):
        wait_in(N, c)
        wait_in(QO, c)
        wait_in(Z4, c)
        wait_in(PO, c)
        for i in range(3):
            big_load(c, i).wait()

        def heads(ref):
            return jnp.concatenate([ref[c, :, h * F : (h + 1) * F] for h in range(GROUP)], axis=0)

        q = heads(qs)
        g = heads(gs)
        o = heads(os)

        def pairs(i):
            out = [noisy[c, :, i].reshape(2 * TOK, F)]
            for d in range(4):
                out.append(jnp.concatenate([win[c, 2 * d, i], win[c, 2 * d + 1, i]], axis=0))
            return out

        keys = pairs(0)
        values = pairs(1)
        prod = g.astype(F32) * o.astype(F32)
        high = prod.astype(BF)
        low = (prod - high.astype(F32)).astype(BF)
        ones = jnp.ones((16, F), BF)
        delta = (dot(ones, high, 1, 1) + dot(ones, low, 1, 1))[0:1]

        const = SCALE * LOG2E
        scores = [dot(k, q, 1, 1) for k in keys]
        tops = [s.max(axis=0, keepdims=True) * const for s in scores]
        top = tops[0]
        for d in range(4):
            top = jnp.maximum(top, tops[d + 1] + bias[d])
        exps = []
        total = jnp.zeros((1, ROWS), F32)
        for d, s in enumerate(scores):
            shift = top if d == 0 else top - bias[d - 1]
            e = jnp.exp2(s * const - shift)
            total = total + e.sum(axis=0, keepdims=True)
            exps.append(e)
        inv = 1.0 / total
        dq = jnp.zeros((F, ROWS), F32)
        for d in range(5):
            p = exps[d] * inv
            dp = dot(values[d], g, 1, 1)
            ds = (p * (dp - delta)).astype(BF)
            dq = dq + dot(keys[d], ds, 0, 0)
            dk = dot(ds, q, 1, 0) * SCALE
            dv = dot(p.astype(BF), g, 1, 0)
            if d == 0:
                own_n[c, 0] = dk[:TOK]
                own_n[c, 1] = dv[:TOK]
                part[c, 8, 0] = dk[TOK:].astype(BF)
                part[c, 8, 1] = dv[TOK:].astype(BF)
            else:
                s0 = 2 * (d - 1)
                part[c, s0, 0] = dk[:TOK].astype(BF)
                part[c, s0, 1] = dv[:TOK].astype(BF)
                part[c, s0 + 1, 0] = dk[TOK:].astype(BF)
                part[c, s0 + 1, 1] = dv[TOK:].astype(BF)
        dq = (dq.T * SCALE).astype(BF)
        for h in range(GROUP):
            dqs[c, :, h * F : (h + 1) * F] = dq[h * TOK : (h + 1) * TOK]
        start_out(PO, c)
        start_out(QO, c)
        start_out(Z4, c)
        start_out(N, c)
        dq_copy(c).start()

    def wide(ref, *index):
        return ref[index].astype(F32)

    def second_out(c):
        for m in (PO, QO, Z4):
            wait_out(m, c)
        part[c, 2 + other] = (wide(part, c, 2 + other) + wide(land, c, QO) + wide(land, c, Z4)).astype(BF)
        s = 2 * (2 - 2 * r) + other
        part[c, s] = (wide(part, c, s) + wide(land, c, PO)).astype(BF)
        start_out(S1, c)
        start_out(S3, c)
        start_out(B2, c)

    def third_out(c):
        for m in (S1, S3, B2):
            wait_out(m, c)
        first = wide(land, c, S1)
        third = wide(land, c, S3)
        part[c, 2 + par] = (
            wide(part, c, 2 + par) + wide(land, c, B2) + jnp.where(r == 1, first, third)
        ).astype(BF)
        start_out(Z1, c)
        part[c, 6 + par] = (wide(part, c, 6 + par) + jnp.where(r == 1, third, 0.0)).astype(BF)
        start_out(Z2, c)

    def last_out(c):
        for m in (N, Z1, Z2):
            wait_out(m, c)
        cols = pl.ds(pl.multiple_of(c * F, F), F)
        clean = wide(land, c, Z1) + wide(land, c, Z2) + jnp.where(r == 0, wide(land, c, S1), 0.0)
        ck_out[0, :, cols] = clean[0].astype(BF)
        cv_out[0, :, cols] = clean[1].astype(BF)
        dirty = own_n[c] + wide(land, c, N)
        nk_out[0, :, cols] = dirty[0].astype(BF)
        nv_out[0, :, cols] = dirty[1].astype(BF)

    pl.semaphore_wait(barrier, 8)
    AHEAD = 2
    for c in range(AHEAD):
        first_hop(c)

    stages = (second_hop, third_hop, compute, second_out, third_out, last_out)

    def step(k, _):
        pl.when(k + AHEAD < CHUNKS)(lambda: first_hop(k + AHEAD))
        for lag, stage in enumerate(stages):
            pl.when((k >= lag) & (k - lag < CHUNKS))(functools.partial(stage, k - lag))
        return 0

    lax.fori_loop(0, CHUNKS + len(stages) - 1, step, 0)

    def drain(c, _):
        dq_copy(c).wait()
        for m in range(9):
            guarded(SENDS_IN, m, lambda: msg_in(m, c).wait_send())
            guarded(SENDS_OUT, m, lambda: msg_out(m, c).wait_send())
        return 0

    lax.fori_loop(0, CHUNKS, drain, 0)


def per_device(noisy_q, noisy_k, noisy_v, clean_k, clean_v, noisy_o, out_grad, block_mask):
    kv = jax.ShapeDtypeStruct(noisy_k.shape, BF)
    hbm = pl.BlockSpec(memory_space=pl.ANY)
    vmem = pl.BlockSpec(memory_space=pltpu.VMEM)
    dma = pltpu.SemaphoreType.DMA
    wide = (CHUNKS, TOK, GROUP * F)
    return pl.pallas_call(
        body,
        out_shape=(jax.ShapeDtypeStruct(noisy_q.shape, BF), kv, kv, kv, kv),
        in_specs=[hbm] * 7 + [pl.BlockSpec(memory_space=pltpu.SMEM)],
        out_specs=(hbm, vmem, vmem, vmem, vmem),
        scratch_shapes=[
            pltpu.VMEM(wide, BF),
            pltpu.VMEM(wide, BF),
            pltpu.VMEM(wide, BF),
            pltpu.VMEM((CHUNKS, 9, 2, TOK, F), BF),
            pltpu.VMEM((CHUNKS, 2, 2, TOK, F), BF),
            pltpu.VMEM((CHUNKS, 9, 2, TOK, F), BF),
            pltpu.VMEM((CHUNKS, 2, TOK, F), F32),
            pltpu.VMEM((CHUNKS, 9, 2, TOK, F), BF),
            pltpu.VMEM(wide, BF),
            dma((CHUNKS, 3)),
            dma((CHUNKS, 4)),
            dma((9, CHUNKS)),
            dma((9, CHUNKS)),
            dma((9, CHUNKS)),
            dma((9, CHUNKS)),
            dma((CHUNKS,)),
            dma((CHUNKS,)),
        ],
        compiler_params=pltpu.CompilerParams(
            collective_id=0, has_side_effects=True, vmem_limit_bytes=48 << 20
        ),
        cost_estimate=pl.CostEstimate(flops=3400000000, bytes_accessed=6 << 20, transcendentals=2700000),
    )(noisy_q, noisy_k, noisy_v, clean_k, clean_v, noisy_o, out_grad, block_mask)


def solution(mesh):
    three = P("pipe", "seq", None)
    return jax.shard_map(
        per_device, mesh=mesh, in_specs=(three,) * 7 + (P("pipe", None, None),), out_specs=(three,) * 5,
        check_vma=False,
    )
```

```python
import functools
import math

import jax
import jax.numpy as jnp
from jax import lax
from jax.experimental import pallas as pl
from jax.experimental.pallas import tpu as pltpu
from jax.sharding import PartitionSpec as P

F = 128
GROUP = 8
CHUNKS = 8
LEVELS = 16
BLOCKS = 32
TOK = 64
ROWS = GROUP * TOK
SCALE = 1.0 / math.sqrt(F)
LOG2E = 1.4426950408889634
MESH = pl.DeviceIdType.MESH
BF = jnp.bfloat16
F32 = jnp.float32

N, Z1, Z2, Z4, B2, S1, S3, QO, PO = range(9)


def dot(a, b, ca, cb):
    return lax.dot_general(a, b, (((ca,), (cb,)), ((), ())), preferred_element_type=F32)


def body(
    q_in, kn_in, vn_in, kc_in, vc_in, o_in, g_in, mask_in,
    pg_out, nk_out, nv_out, ck_out, cv_out,
    mask, mask_sem, qs, gs, os, win, noisy, part, own_n, land, dqs,
    big_sem, kv_sem, in_send, in_recv, out_send, out_recv, dq_send, dq_recv,
):
    seq = lax.axis_index("seq")
    pipe = lax.axis_index("pipe")
    lev = seq // 4
    x = seq % 4
    r = x // 2
    par = x % 2
    other = 1 - par
    blk = 2 * lev + r

    mate = (lev * 4 + r * 2 + other, pipe)
    inter = (lev * 4 + 3 - x, pipe)

    def level(step):
        return (((lev + step + LEVELS) % LEVELS) * 4 + x, pipe)

    up1, up2, down1, down2 = level(1), level(2), level(-1), level(-2)
    pipe_to = (seq, (pipe + 3) % 4)
    pipe_from = (seq, (pipe + 1) % 4)

    barrier = pltpu.get_barrier_semaphore()
    for device in (mate, inter, up1, up2, down1, down2, pipe_to, pipe_from):
        pl.semaphore_signal(barrier, inc=1, device_id=device, device_id_type=MESH)

    def kv_load(c, i):
        src = (kc_in, vc_in, kn_in, vn_in)[i]
        dst = (win.at[c, 8, 0], win.at[c, 8, 1], noisy.at[c, 0, 0], noisy.at[c, 0, 1])[i]
        cols = pl.ds(pl.multiple_of(c * F, F), F)
        return pltpu.make_async_copy(src.at[0, :, cols], dst, kv_sem.at[c, i])

    def big_load(c, i):
        src = (q_in, g_in, o_in)[i]
        dst = (qs, gs, os)[i].at[c]
        cols = pl.ds(pl.multiple_of(c * GROUP * F, F), GROUP * F)
        return pltpu.make_async_copy(src.at[0, :, cols], dst, big_sem.at[c, i])

    def load_kv(c, _):
        for i in range(4):
            kv_load(c, i).start()
        return 0

    def load_big(c, _):
        for i in range(3):
            big_load(c, i).start()
        return 0

    mask_load = pltpu.make_async_copy(mask_in, mask, mask_sem)
    mask_load.start()
    lax.fori_loop(0, CHUNKS, load_kv, 0)
    lax.fori_loop(0, CHUNKS, load_big, 0)

    zero = jnp.zeros((2, TOK, F), BF)

    def clear(pred, ref, slots):
        @pl.when(pred)
        def _():
            def one(c, _):
                for s in slots:
                    ref[c, s] = zero
                return 0

            lax.fori_loop(0, CHUNKS, one, 0)

    clear(lev < 1, win, (2 + par, 6 + other))
    clear(lev < 2, win, (6 + par,))
    clear(lev > LEVELS - 2, land, (Z1, Z4))
    clear(lev > LEVELS - 3, land, (Z2,))

    def send_in(m, c, src, dst, device):
        return pltpu.make_async_remote_copy(
            src_ref=src, dst_ref=dst, send_sem=in_send.at[m, c], recv_sem=in_recv.at[m, c],
            device_id=device, device_id_type=MESH,
        )

    def slot(c, d, p):
        return win.at[c, 2 * d + p]

    def msg_in(m, c):
        if m == N:
            return send_in(m, c, noisy.at[c, 0], noisy.at[c, 1], mate)
        if m == Z1:
            return send_in(m, c, win.at[c, 8], slot(c, 1, par), up1)
        if m == Z2:
            return send_in(m, c, win.at[c, 8], slot(c, 3, par), up2)
        if m == Z4:
            return send_in(m, c, slot(c, 1, other), slot(c, 3, other), up1)
        if m == B2:
            return send_in(m, c, slot(c, 1, par), slot(c, 1, par), mate)
        if m == S1:
            return send_in(m, c, win.at[c, 8 - r * (6 - par)], slot(c, 0, par), inter)
        if m == S3:
            return send_in(m, c, slot(c, 1 + 2 * r, par), slot(c, 2, par), inter)
        if m == QO:
            return send_in(m, c, slot(c, 1, other), slot(c, 2 - 2 * r, other), inter)
        return send_in(m, c, slot(c, 2 - 2 * r, other), slot(c, 2 - 2 * r, other), mate)

    def msg_out(m, c):
        src = {
            N: part.at[c, 8],
            PO: part.at[c, 2 * (2 - 2 * r) + par],
            QO: part.at[c, 2 * (2 * r) + par],
            Z4: part.at[c, 6 + other],
            B2: part.at[c, 2 + other],
            S1: part.at[c, 0 + other],
            S3: part.at[c, 4 + other],
            Z1: part.at[c, 2 + par],
            Z2: part.at[c, 6 + par],
        }[m]
        device = {
            N: mate, PO: mate, B2: mate, QO: inter, S1: inter, S3: inter,
            Z4: down1, Z1: down1, Z2: down2,
        }[m]
        return pltpu.make_async_remote_copy(
            src_ref=src, dst_ref=land.at[c, m], send_sem=out_send.at[m, c], recv_sem=out_recv.at[m, c],
            device_id=device, device_id_type=MESH,
        )

    def dq_copy(c):
        cols = pl.ds(pl.multiple_of(c * GROUP * F, F), GROUP * F)
        return pltpu.make_async_remote_copy(
            src_ref=dqs.at[c], dst_ref=pg_out.at[0, :, cols], send_sem=dq_send.at[c], recv_sem=dq_recv.at[c],
            device_id=pipe_to, device_id_type=MESH,
        )

    SENDS_IN = {Z1: lev < LEVELS - 1, Z2: lev < LEVELS - 2, Z4: lev < LEVELS - 1}
    GETS_IN = {Z1: lev > 0, Z2: lev > 1, Z4: lev > 0}
    SENDS_OUT, GETS_OUT = GETS_IN, SENDS_IN

    def guarded(table, m, act):
        if m in table:
            pl.when(table[m])(act)
        else:
            act()

    def start_in(m, c):
        guarded(SENDS_IN, m, lambda: msg_in(m, c).start())

    def wait_in(m, c):
        guarded(GETS_IN, m, lambda: msg_in(m, c).wait_recv())

    def start_out(m, c):
        guarded(SENDS_OUT, m, lambda: msg_out(m, c).start())

    def wait_out(m, c):
        guarded(GETS_OUT, m, lambda: msg_out(m, c).wait_recv())

    def first_hop(c):
        for i in range(4):
            kv_load(c, i).wait()
        start_in(Z1, c)
        start_in(N, c)

        @pl.when(r == 0)
        def _():
            start_in(S1, c)

        start_in(Z2, c)

    def second_hop(c):
        wait_in(Z1, c)
        start_in(B2, c)

        @pl.when(r == 1)
        def _():
            start_in(S1, c)

        wait_in(Z2, c)
        start_in(S3, c)

    def third_hop(c):
        wait_in(B2, c)
        start_in(QO, c)
        start_in(Z4, c)
        wait_in(S1, c)
        wait_in(S3, c)
        start_in(PO, c)

    mask_load.wait()
    bias = []
    for d in range(4):
        flag = mask[0, blk, (blk + BLOCKS - 1 - d) % BLOCKS]
        bias.append(jnp.where((blk - 1 - d >= 0) & (flag == 1), jnp.float32(0.0), jnp.float32(-1e30)))

    def compute(c):
        wait_in(N, c)
        wait_in(QO, c)
        wait_in(Z4, c)
        wait_in(PO, c)
        for i in range(3):
            big_load(c, i).wait()

        def heads(ref):
            return jnp.concatenate([ref[c, :, h * F : (h + 1) * F] for h in range(GROUP)], axis=0)

        q = heads(qs)
        g = heads(gs)
        o = heads(os)

        def pairs(i):
            out = [noisy[c, :, i].reshape(2 * TOK, F)]
            for d in range(4):
                out.append(jnp.concatenate([win[c, 2 * d, i], win[c, 2 * d + 1, i]], axis=0))
            return out

        keys = pairs(0)
        values = pairs(1)
        prod = g.astype(F32) * o.astype(F32)
        high = prod.astype(BF)
        low = (prod - high.astype(F32)).astype(BF)
        ones = jnp.ones((16, F), BF)
        delta = (dot(ones, high, 1, 1) + dot(ones, low, 1, 1))[0:1]

        const = SCALE * LOG2E
        scores = [dot(k, q, 1, 1) for k in keys]
        tops = [s.max(axis=0, keepdims=True) * const for s in scores]
        top = tops[0]
        for d in range(4):
            top = jnp.maximum(top, tops[d + 1] + bias[d])
        exps = []
        total = jnp.zeros((1, ROWS), F32)
        for d, s in enumerate(scores):
            shift = top if d == 0 else top - bias[d - 1]
            e = jnp.exp2(s * const - shift)
            total = total + e.sum(axis=0, keepdims=True)
            exps.append(e)
        inv = 1.0 / total
        dq = jnp.zeros((F, ROWS), F32)
        for d in range(5):
            p = exps[d] * inv
            dp = dot(values[d], g, 1, 1)
            ds = (p * (dp - delta)).astype(BF)
            dq = dq + dot(keys[d], ds, 0, 0)
            dk = dot(ds, q, 1, 0) * SCALE
            dv = dot(p.astype(BF), g, 1, 0)
            if d == 0:
                own_n[c, 0] = dk[:TOK]
                own_n[c, 1] = dv[:TOK]
                part[c, 8, 0] = dk[TOK:].astype(BF)
                part[c, 8, 1] = dv[TOK:].astype(BF)
            else:
                s0 = 2 * (d - 1)
                part[c, s0, 0] = dk[:TOK].astype(BF)
                part[c, s0, 1] = dv[:TOK].astype(BF)
                part[c, s0 + 1, 0] = dk[TOK:].astype(BF)
                part[c, s0 + 1, 1] = dv[TOK:].astype(BF)
        dq = (dq.T * SCALE).astype(BF)
        for h in range(GROUP):
            dqs[c, :, h * F : (h + 1) * F] = dq[h * TOK : (h + 1) * TOK]
        start_out(PO, c)
        start_out(QO, c)
        start_out(Z4, c)
        start_out(N, c)
        dq_copy(c).start()

    def wide(ref, *index):
        return ref[index].astype(F32)

    def second_out(c):
        for m in (PO, QO, Z4):
            wait_out(m, c)
        part[c, 2 + other] = (wide(part, c, 2 + other) + wide(land, c, QO) + wide(land, c, Z4)).astype(BF)
        s = 2 * (2 - 2 * r) + other
        part[c, s] = (wide(part, c, s) + wide(land, c, PO)).astype(BF)
        start_out(S1, c)
        start_out(S3, c)
        start_out(B2, c)

    def third_out(c):
        for m in (S1, S3, B2):
            wait_out(m, c)
        first = wide(land, c, S1)
        third = wide(land, c, S3)
        part[c, 2 + par] = (
            wide(part, c, 2 + par) + wide(land, c, B2) + jnp.where(r == 1, first, third)
        ).astype(BF)
        start_out(Z1, c)
        part[c, 6 + par] = (wide(part, c, 6 + par) + jnp.where(r == 1, third, 0.0)).astype(BF)
        start_out(Z2, c)

    def last_out(c):
        for m in (N, Z1, Z2):
            wait_out(m, c)
        cols = pl.ds(pl.multiple_of(c * F, F), F)
        clean = wide(land, c, Z1) + wide(land, c, Z2) + jnp.where(r == 0, wide(land, c, S1), 0.0)
        ck_out[0, :, cols] = clean[0].astype(BF)
        cv_out[0, :, cols] = clean[1].astype(BF)
        dirty = own_n[c] + wide(land, c, N)
        nk_out[0, :, cols] = dirty[0].astype(BF)
        nv_out[0, :, cols] = dirty[1].astype(BF)

    pl.semaphore_wait(barrier, 8)
    for c in range(2):
        first_hop(c)

    def stage(k, fn, lag, rate):
        for b in range(rate):
            c = rate * (k - lag) + b
            pl.when((c >= 0) & (c < CHUNKS))(functools.partial(fn, c))

    def step(k, _):
        pl.when(k + 2 < CHUNKS)(lambda: first_hop(k + 2))
        stage(k, second_hop, 0, 1)
        stage(k, third_hop, 2, 1)
        stage(k, compute, 4, 1)
        stage(k, second_out, 6, 1)
        stage(k, third_out, 8, 1)
        stage(k, last_out, 10, 1)
        return 0

    lax.fori_loop(0, CHUNKS + 10, step, 0)

    def drain(c, _):
        dq_copy(c).wait()
        for m in range(9):
            guarded(SENDS_IN, m, lambda: msg_in(m, c).wait_send())
            guarded(SENDS_OUT, m, lambda: msg_out(m, c).wait_send())
        return 0

    lax.fori_loop(0, CHUNKS, drain, 0)


def finish(*refs):
    copies = [pltpu.make_async_copy(refs[i], refs[5 + i], refs[10].at[i]) for i in range(5)]
    for copy in copies:
        copy.start()
    for copy in copies:
        copy.wait()


def per_device(*args):
    noisy_q, noisy_k = args[:2]
    kv = jax.ShapeDtypeStruct(noisy_k.shape, BF)
    hbm = pl.BlockSpec(memory_space=pltpu.HBM)
    vmem = pl.BlockSpec(memory_space=pltpu.VMEM)
    dma = pltpu.SemaphoreType.DMA
    wide = (CHUNKS, TOK, GROUP * F)
    outs = pl.pallas_call(
        body,
        out_shape=(pltpu.VMEM(noisy_q.shape, BF),) + (pltpu.VMEM(noisy_k.shape, BF),) * 4,
        in_specs=[hbm] * 8,
        out_specs=(vmem,) * 5,
        scratch_shapes=[
            pltpu.SMEM((1, BLOCKS, BLOCKS), jnp.int32),
            dma(()),
            pltpu.VMEM(wide, BF),
            pltpu.VMEM(wide, BF),
            pltpu.VMEM(wide, BF),
            pltpu.VMEM((CHUNKS, 9, 2, TOK, F), BF),
            pltpu.VMEM((CHUNKS, 2, 2, TOK, F), BF),
            pltpu.VMEM((CHUNKS, 9, 2, TOK, F), BF),
            pltpu.VMEM((CHUNKS, 2, TOK, F), F32),
            pltpu.VMEM((CHUNKS, 9, 2, TOK, F), BF),
            pltpu.VMEM(wide, BF),
            dma((CHUNKS, 3)),
            dma((CHUNKS, 4)),
            dma((9, CHUNKS)),
            dma((9, CHUNKS)),
            dma((9, CHUNKS)),
            dma((9, CHUNKS)),
            dma((CHUNKS,)),
            dma((CHUNKS,)),
        ],
        compiler_params=pltpu.CompilerParams(
            collective_id=0, has_side_effects=True, vmem_limit_bytes=40 << 20
        ),
        cost_estimate=pl.CostEstimate(flops=3400000000, bytes_accessed=6 << 20, transcendentals=2700000),
    )(*[pltpu.with_memory_space_constraint(a, pltpu.HBM) for a in args])
    return pl.pallas_call(
        finish,
        out_shape=(jax.ShapeDtypeStruct(noisy_q.shape, BF), kv, kv, kv, kv),
        in_specs=[vmem] * 5,
        out_specs=(hbm,) * 5,
        scratch_shapes=[dma((5,))],
        compiler_params=pltpu.CompilerParams(vmem_limit_bytes=8 << 20),
    )(*outs)


def solution(mesh):
    three = P("pipe", "seq", None)
    return jax.shard_map(
        per_device, mesh=mesh, in_specs=(three,) * 7 + (P("pipe", None, None),), out_specs=(three,) * 5,
        check_vma=False,
    )
```

```python
import functools
import math

import jax
import jax.numpy as jnp
from jax import lax
from jax.experimental import pallas as pl
from jax.experimental.pallas import tpu as pltpu
from jax.sharding import PartitionSpec as P

F = 128
GROUP = 8
CHUNKS = 8
LEVELS = 16
BLOCKS = 32
TOK = 64
ROWS = GROUP * TOK
SCALE = 1.0 / math.sqrt(F)
LOG2E = 1.4426950408889634
MESH = pl.DeviceIdType.MESH
BF = jnp.bfloat16
F32 = jnp.float32

N, Z1, Z2, Z4, B2, S1, S3, QO, PO = range(9)


def dot(a, b, ca, cb):
    return lax.dot_general(a, b, (((ca,), (cb,)), ((), ())), preferred_element_type=F32)


def body(
    q_in, kn_in, vn_in, kc_in, vc_in, o_in, g_in, mask_in,
    pg_out, nk_out, nv_out, ck_out, cv_out,
    mask, mask_sem, qs, gs, os, win, noisy, part, own_n, land, dqs,
    big_sem, kv_sem, in_send, in_recv, out_send, out_recv, dq_send, dq_recv,
):
    seq = lax.axis_index("seq")
    pipe = lax.axis_index("pipe")
    lev = seq // 4
    x = seq % 4
    r = x // 2
    par = x % 2
    other = 1 - par
    blk = 2 * lev + r

    mate = (lev * 4 + r * 2 + other, pipe)
    inter = (lev * 4 + 3 - x, pipe)

    def level(step):
        return (((lev + step + LEVELS) % LEVELS) * 4 + x, pipe)

    up1, up2, down1, down2 = level(1), level(2), level(-1), level(-2)
    pipe_to = (seq, (pipe + 3) % 4)
    pipe_from = (seq, (pipe + 1) % 4)

    barrier = pltpu.get_barrier_semaphore()
    for device in (mate, inter, up1, up2, down1, down2, pipe_to, pipe_from):
        pl.semaphore_signal(barrier, inc=1, device_id=device, device_id_type=MESH)

    def kv_load(c, i):
        src = (kc_in, vc_in, kn_in, vn_in)[i]
        dst = (win.at[c, 8, 0], win.at[c, 8, 1], noisy.at[c, 0, 0], noisy.at[c, 0, 1])[i]
        cols = pl.ds(pl.multiple_of(c * F, F), F)
        return pltpu.make_async_copy(src.at[0, :, cols], dst, kv_sem.at[c, i])

    def big_load(c, i):
        src = (q_in, g_in, o_in)[i]
        dst = (qs, gs, os)[i].at[c]
        cols = pl.ds(pl.multiple_of(c * GROUP * F, F), GROUP * F)
        return pltpu.make_async_copy(src.at[0, :, cols], dst, big_sem.at[c, i])

    def load_kv(c, _):
        for i in range(4):
            kv_load(c, i).start()
        return 0

    def load_big(c, _):
        for i in range(3):
            big_load(c, i).start()
        return 0

    mask_load = pltpu.make_async_copy(mask_in, mask, mask_sem)
    mask_load.start()
    AHEAD = 2
    for c in range(AHEAD):
        load_kv(c, 0)

    zero = jnp.zeros((2, TOK, F), BF)

    def clear(pred, ref, slots):
        @pl.when(pred)
        def _():
            def one(c, _):
                for s in slots:
                    ref[c, s] = zero
                return 0

            lax.fori_loop(0, CHUNKS, one, 0)

    clear(lev < 1, win, (2 + par, 6 + other))
    clear(lev < 2, win, (6 + par,))
    clear(lev > LEVELS - 2, land, (Z1, Z4))
    clear(lev > LEVELS - 3, land, (Z2,))

    def send_in(m, c, src, dst, device):
        return pltpu.make_async_remote_copy(
            src_ref=src, dst_ref=dst, send_sem=in_send.at[m, c], recv_sem=in_recv.at[m, c],
            device_id=device, device_id_type=MESH,
        )

    def slot(c, d, p):
        return win.at[c, 2 * d + p]

    def msg_in(m, c):
        if m == N:
            return send_in(m, c, noisy.at[c, 0], noisy.at[c, 1], mate)
        if m == Z1:
            return send_in(m, c, win.at[c, 8], slot(c, 1, par), up1)
        if m == Z2:
            return send_in(m, c, win.at[c, 8], slot(c, 3, par), up2)
        if m == Z4:
            return send_in(m, c, slot(c, 1, other), slot(c, 3, other), up1)
        if m == B2:
            return send_in(m, c, slot(c, 1, par), slot(c, 1, par), mate)
        if m == S1:
            return send_in(m, c, win.at[c, 8 - r * (6 - par)], slot(c, 0, par), inter)
        if m == S3:
            return send_in(m, c, slot(c, 1 + 2 * r, par), slot(c, 2, par), inter)
        if m == QO:
            return send_in(m, c, slot(c, 1, other), slot(c, 2 - 2 * r, other), inter)
        return send_in(m, c, slot(c, 2 - 2 * r, other), slot(c, 2 - 2 * r, other), mate)

    def msg_out(m, c):
        src = {
            N: part.at[c, 8],
            PO: part.at[c, 2 * (2 - 2 * r) + par],
            QO: part.at[c, 2 * (2 * r) + par],
            Z4: part.at[c, 6 + other],
            B2: part.at[c, 2 + other],
            S1: part.at[c, 0 + other],
            S3: part.at[c, 4 + other],
            Z1: part.at[c, 2 + par],
            Z2: part.at[c, 6 + par],
        }[m]
        device = {
            N: mate, PO: mate, B2: mate, QO: inter, S1: inter, S3: inter,
            Z4: down1, Z1: down1, Z2: down2,
        }[m]
        return pltpu.make_async_remote_copy(
            src_ref=src, dst_ref=land.at[c, m], send_sem=out_send.at[m, c], recv_sem=out_recv.at[m, c],
            device_id=device, device_id_type=MESH,
        )

    def dq_copy(c):
        cols = pl.ds(pl.multiple_of(c * GROUP * F, F), GROUP * F)
        return pltpu.make_async_remote_copy(
            src_ref=dqs.at[c], dst_ref=pg_out.at[0, :, cols], send_sem=dq_send.at[c], recv_sem=dq_recv.at[c],
            device_id=pipe_to, device_id_type=MESH,
        )

    SENDS_IN = {Z1: lev < LEVELS - 1, Z2: lev < LEVELS - 2, Z4: lev < LEVELS - 1}
    GETS_IN = {Z1: lev > 0, Z2: lev > 1, Z4: lev > 0}
    SENDS_OUT, GETS_OUT = GETS_IN, SENDS_IN

    def guarded(table, m, act):
        if m in table:
            pl.when(table[m])(act)
        else:
            act()

    def start_in(m, c):
        guarded(SENDS_IN, m, lambda: msg_in(m, c).start())

    def wait_in(m, c):
        guarded(GETS_IN, m, lambda: msg_in(m, c).wait_recv())

    def start_out(m, c):
        guarded(SENDS_OUT, m, lambda: msg_out(m, c).start())

    def wait_out(m, c):
        guarded(GETS_OUT, m, lambda: msg_out(m, c).wait_recv())

    def first_hop(c):
        for i in range(4):
            kv_load(c, i).wait()
        start_in(Z1, c)
        start_in(N, c)

        @pl.when(r == 0)
        def _():
            start_in(S1, c)

        start_in(Z2, c)

    def second_hop(c):
        wait_in(Z1, c)
        start_in(B2, c)

        @pl.when(r == 1)
        def _():
            start_in(S1, c)

        wait_in(Z2, c)
        start_in(S3, c)

    def third_hop(c):
        wait_in(B2, c)
        start_in(QO, c)
        start_in(Z4, c)
        wait_in(S1, c)
        wait_in(S3, c)
        start_in(PO, c)

    mask_load.wait()
    bias = []
    for d in range(4):
        flag = mask[0, blk, (blk + BLOCKS - 1 - d) % BLOCKS]
        bias.append(jnp.where((blk - 1 - d >= 0) & (flag == 1), jnp.float32(0.0), jnp.float32(-1e30)))

    def compute(c):
        wait_in(N, c)
        wait_in(QO, c)
        wait_in(Z4, c)
        wait_in(PO, c)
        for i in range(3):
            big_load(c, i).wait()

        def heads(ref):
            return jnp.concatenate([ref[c, :, h * F : (h + 1) * F] for h in range(GROUP)], axis=0)

        q = heads(qs)
        g = heads(gs)
        o = heads(os)

        def pairs(i):
            out = [noisy[c, :, i].reshape(2 * TOK, F)]
            for d in range(4):
                out.append(jnp.concatenate([win[c, 2 * d, i], win[c, 2 * d + 1, i]], axis=0))
            return out

        keys = pairs(0)
        values = pairs(1)
        prod = g.astype(F32) * o.astype(F32)
        high = prod.astype(BF)
        low = (prod - high.astype(F32)).astype(BF)
        ones = jnp.ones((16, F), BF)
        delta = (dot(ones, high, 1, 1) + dot(ones, low, 1, 1))[0:1]

        const = SCALE * LOG2E
        scores = [dot(k, q, 1, 1) for k in keys]
        tops = [s.max(axis=0, keepdims=True) * const for s in scores]
        top = tops[0]
        for d in range(4):
            top = jnp.maximum(top, tops[d + 1] + bias[d])
        exps = []
        total = jnp.zeros((1, ROWS), F32)
        for d, s in enumerate(scores):
            shift = top if d == 0 else top - bias[d - 1]
            e = jnp.exp2(s * const - shift)
            total = total + e.sum(axis=0, keepdims=True)
            exps.append(e)
        inv = 1.0 / total
        dq = jnp.zeros((F, ROWS), F32)
        for d in (1, 3, 4, 0, 2):
            p = exps[d] * inv
            dp = dot(values[d], g, 1, 1)
            ds = (p * (dp - delta)).astype(BF)
            dq = dq + dot(keys[d], ds, 0, 0)
            dk = dot(ds, q, 1, 0) * SCALE
            dv = dot(p.astype(BF), g, 1, 0)
            if d == 0:
                own_n[c, 0] = dk[:TOK]
                own_n[c, 1] = dv[:TOK]
                part[c, 8, 0] = dk[TOK:].astype(BF)
                part[c, 8, 1] = dv[TOK:].astype(BF)
            else:
                s0 = 2 * (d - 1)
                part[c, s0, 0] = dk[:TOK].astype(BF)
                part[c, s0, 1] = dv[:TOK].astype(BF)
                part[c, s0 + 1, 0] = dk[TOK:].astype(BF)
                part[c, s0 + 1, 1] = dv[TOK:].astype(BF)
            if d == 3:
                start_out(PO, c)
                start_out(QO, c)
                pl.when(r == 0)(lambda: start_out(S1, c))
                pl.when(r == 1)(lambda: start_out(S3, c))
            elif d == 4:
                start_out(Z4, c)
                pl.when(r == 0)(lambda: start_out(Z2, c))
            elif d == 0:
                start_out(N, c)
        dq = (dq.T * SCALE).astype(BF)
        for h in range(GROUP):
            dqs[c, :, h * F : (h + 1) * F] = dq[h * TOK : (h + 1) * TOK]
        dq_copy(c).start()

    def wide(ref, *index):
        return ref[index].astype(F32)

    def second_out(c):
        for m in range(9):
            guarded(SENDS_IN, m, lambda: msg_in(m, c).wait_send())
        for m in (PO, QO, Z4):
            wait_out(m, c)
        part[c, 2 + other] = (wide(part, c, 2 + other) + wide(land, c, QO) + wide(land, c, Z4)).astype(BF)
        s = 2 * (2 - 2 * r) + other
        part[c, s] = (wide(part, c, s) + wide(land, c, PO)).astype(BF)
        pl.when(r == 0)(lambda: start_out(S3, c))
        pl.when(r == 1)(lambda: start_out(S1, c))
        start_out(B2, c)

    def third_out(c):
        for m in (S1, S3, B2):
            wait_out(m, c)
        first = wide(land, c, S1)
        third = wide(land, c, S3)
        part[c, 2 + par] = (
            wide(part, c, 2 + par) + wide(land, c, B2) + jnp.where(r == 1, first, third)
        ).astype(BF)
        start_out(Z1, c)

        @pl.when(r == 1)
        def _():
            part[c, 6 + par] = (wide(part, c, 6 + par) + third).astype(BF)
            start_out(Z2, c)

    def last_out(c):
        for m in (N, Z1, Z2):
            wait_out(m, c)
        cols = pl.ds(pl.multiple_of(c * F, F), F)
        clean = wide(land, c, Z1) + wide(land, c, Z2) + jnp.where(r == 0, wide(land, c, S1), 0.0)
        ck_out[0, :, cols] = clean[0].astype(BF)
        cv_out[0, :, cols] = clean[1].astype(BF)
        dirty = own_n[c] + wide(land, c, N)
        nk_out[0, :, cols] = dirty[0].astype(BF)
        nv_out[0, :, cols] = dirty[1].astype(BF)
        dq_copy(c).wait()
        for m in range(9):
            guarded(SENDS_OUT, m, lambda: msg_out(m, c).wait_send())

    pl.semaphore_wait(barrier, 8)
    for c in range(AHEAD):
        first_hop(c)
    lax.fori_loop(AHEAD, CHUNKS, load_kv, 0)
    lax.fori_loop(0, CHUNKS, load_big, 0)

    def stage(k, fn, lag, rate):
        for b in range(rate):
            c = rate * (k - lag) + b
            pl.when((c >= 0) & (c < CHUNKS))(functools.partial(fn, c))

    def step(k, _):
        pl.when(k + AHEAD < CHUNKS)(lambda: first_hop(k + AHEAD))
        stage(k, second_hop, 0, 1)
        stage(k, third_hop, 2, 1)
        stage(k, compute, 4, 1)
        stage(k, second_out, 6, 1)
        stage(k, third_out, 8, 1)
        stage(k, last_out, 10, 1)
        return 0

    lax.fori_loop(0, CHUNKS + 10, step, 0)


def finish(*refs):
    copies = [pltpu.make_async_copy(refs[i], refs[5 + i], refs[10].at[i]) for i in range(5)]
    for copy in copies:
        copy.start()
    for copy in copies:
        copy.wait()


def per_device(*args):
    noisy_q, noisy_k = args[:2]
    kv = jax.ShapeDtypeStruct(noisy_k.shape, BF)
    hbm = pl.BlockSpec(memory_space=pltpu.HBM)
    vmem = pl.BlockSpec(memory_space=pltpu.VMEM)
    dma = pltpu.SemaphoreType.DMA
    wide = (CHUNKS, TOK, GROUP * F)
    outs = pl.pallas_call(
        body,
        out_shape=(pltpu.VMEM(noisy_q.shape, BF),) + (pltpu.VMEM(noisy_k.shape, BF),) * 4,
        in_specs=[hbm] * 8,
        out_specs=(vmem,) * 5,
        scratch_shapes=[
            pltpu.SMEM((1, BLOCKS, BLOCKS), jnp.int32),
            dma(()),
            pltpu.VMEM(wide, BF),
            pltpu.VMEM(wide, BF),
            pltpu.VMEM(wide, BF),
            pltpu.VMEM((CHUNKS, 9, 2, TOK, F), BF),
            pltpu.VMEM((CHUNKS, 2, 2, TOK, F), BF),
            pltpu.VMEM((CHUNKS, 9, 2, TOK, F), BF),
            pltpu.VMEM((CHUNKS, 2, TOK, F), F32),
            pltpu.VMEM((CHUNKS, 9, 2, TOK, F), BF),
            pltpu.VMEM(wide, BF),
            dma((CHUNKS, 3)),
            dma((CHUNKS, 4)),
            dma((9, CHUNKS)),
            dma((9, CHUNKS)),
            dma((9, CHUNKS)),
            dma((9, CHUNKS)),
            dma((CHUNKS,)),
            dma((CHUNKS,)),
        ],
        compiler_params=pltpu.CompilerParams(
            collective_id=0, has_side_effects=True, vmem_limit_bytes=40 << 20
        ),
        cost_estimate=pl.CostEstimate(flops=3400000000, bytes_accessed=6 << 20, transcendentals=2700000),
    )(*[pltpu.with_memory_space_constraint(a, pltpu.HBM) for a in args])
    return pl.pallas_call(
        finish,
        out_shape=(jax.ShapeDtypeStruct(noisy_q.shape, BF), kv, kv, kv, kv),
        in_specs=[vmem] * 5,
        out_specs=(hbm,) * 5,
        scratch_shapes=[dma((5,))],
        compiler_params=pltpu.CompilerParams(vmem_limit_bytes=8 << 20),
    )(*outs)


def solution(mesh):
    three = P("pipe", "seq", None)
    return jax.shard_map(
        per_device, mesh=mesh, in_specs=(three,) * 7 + (P("pipe", None, None),), out_specs=(three,) * 5,
        check_vma=False,
    )
```

```python
import functools
import math

import jax
import jax.numpy as jnp
from jax import lax
from jax.experimental import pallas as pl
from jax.experimental.pallas import tpu as pltpu
from jax.sharding import PartitionSpec as P

F = 128
GROUP = 8
CHUNKS = 8
LEVELS = 16
BLOCKS = 32
TOK = 64
ROWS = GROUP * TOK
SCALE = 1.0 / math.sqrt(F)
LOG2E = 1.4426950408889634
MESH = pl.DeviceIdType.MESH
BF = jnp.bfloat16
F32 = jnp.float32

N, Z1, Z2, Z4, B2, S1, S3, QO, PO = range(9)


def dot(a, b, ca, cb):
    return lax.dot_general(a, b, (((ca,), (cb,)), ((), ())), preferred_element_type=F32)


def body(
    q_in, kn_in, vn_in, kc_in, vc_in, o_in, g_in, mask_in,
    pg_out, nk_out, nv_out, ck_out, cv_out,
    mask, mask_sem, qs, gs, os, win, noisy, part, own_n, land, dqs,
    big_sem, kv_sem, in_send, in_recv, out_send, out_recv, dq_send, dq_recv,
):
    seq = lax.axis_index("seq")
    pipe = lax.axis_index("pipe")
    lev = seq // 4
    x = seq % 4
    r = x // 2
    par = x % 2
    other = 1 - par
    blk = 2 * lev + r

    mate = (lev * 4 + r * 2 + other, pipe)
    inter = (lev * 4 + 3 - x, pipe)

    def level(step):
        return (((lev + step + LEVELS) % LEVELS) * 4 + x, pipe)

    up1, up2, down1, down2 = level(1), level(2), level(-1), level(-2)
    pipe_to = (seq, (pipe + 3) % 4)
    pipe_from = (seq, (pipe + 1) % 4)

    barrier = pltpu.get_barrier_semaphore()
    for device in (mate, inter, up1, up2, down1, down2, pipe_to, pipe_from):
        pl.semaphore_signal(barrier, inc=1, device_id=device, device_id_type=MESH)

    def kv_load(c, i):
        src = (kc_in, vc_in, kn_in, vn_in)[i]
        dst = (win.at[c, 8, 0], win.at[c, 8, 1], noisy.at[c, 0, 0], noisy.at[c, 0, 1])[i]
        cols = pl.ds(pl.multiple_of(c * F, F), F)
        return pltpu.make_async_copy(src.at[0, :, cols], dst, kv_sem.at[c, i])

    def big_load(c, i):
        src = (q_in, g_in, o_in)[i]
        dst = (qs, gs, os)[i].at[c]
        cols = pl.ds(pl.multiple_of(c * GROUP * F, F), GROUP * F)
        return pltpu.make_async_copy(src.at[0, :, cols], dst, big_sem.at[c, i])

    def load_kv(c, _):
        for i in range(4):
            kv_load(c, i).start()
        return 0

    def load_big(c, _):
        for i in range(3):
            big_load(c, i).start()
        return 0

    mask_load = pltpu.make_async_copy(mask_in, mask, mask_sem)
    mask_load.start()
    AHEAD = 2
    for c in range(AHEAD):
        load_kv(c, 0)

    zero = jnp.zeros((2, TOK, F), BF)

    def clear(pred, ref, slots):
        @pl.when(pred)
        def _():
            def one(c, _):
                for s in slots:
                    ref[c, s] = zero
                return 0

            lax.fori_loop(0, CHUNKS, one, 0)

    clear(lev < 1, win, (2 + par, 6 + other))
    clear(lev < 2, win, (6 + par,))
    clear(lev > LEVELS - 2, land, (Z1, Z4))
    clear(lev > LEVELS - 3, land, (Z2,))

    def send_in(m, c, src, dst, device):
        return pltpu.make_async_remote_copy(
            src_ref=src, dst_ref=dst, send_sem=in_send.at[m, c], recv_sem=in_recv.at[m, c],
            device_id=device, device_id_type=MESH,
        )

    def slot(c, d, p):
        return win.at[c, 2 * d + p]

    def msg_in(m, c):
        if m == N:
            return send_in(m, c, noisy.at[c, 0], noisy.at[c, 1], mate)
        if m == Z1:
            return send_in(m, c, win.at[c, 8], slot(c, 1, par), up1)
        if m == Z2:
            return send_in(m, c, win.at[c, 8], slot(c, 3, par), up2)
        if m == Z4:
            return send_in(m, c, slot(c, 1, other), slot(c, 3, other), up1)
        if m == B2:
            return send_in(m, c, slot(c, 1, par), slot(c, 1, par), mate)
        if m == S1:
            return send_in(m, c, win.at[c, 8 - r * (6 - par)], slot(c, 0, par), inter)
        if m == S3:
            return send_in(m, c, slot(c, 1 + 2 * r, par), slot(c, 2, par), inter)
        if m == QO:
            return send_in(m, c, slot(c, 1, other), slot(c, 2 - 2 * r, other), inter)
        return send_in(m, c, slot(c, 2 - 2 * r, other), slot(c, 2 - 2 * r, other), mate)

    def msg_out(m, c):
        src = {
            N: part.at[c, 8],
            PO: part.at[c, 2 * (2 - 2 * r) + par],
            QO: part.at[c, 2 * (2 * r) + par],
            Z4: part.at[c, 6 + other],
            B2: part.at[c, 2 + other],
            S1: part.at[c, 0 + other],
            S3: part.at[c, 4 + other],
            Z1: part.at[c, 2 + par],
            Z2: part.at[c, 6 + par],
        }[m]
        device = {
            N: mate, PO: mate, B2: mate, QO: inter, S1: inter, S3: inter,
            Z4: down1, Z1: down1, Z2: down2,
        }[m]
        return pltpu.make_async_remote_copy(
            src_ref=src, dst_ref=land.at[c, m], send_sem=out_send.at[m, c], recv_sem=out_recv.at[m, c],
            device_id=device, device_id_type=MESH,
        )

    def dq_copy(c):
        cols = pl.ds(pl.multiple_of(c * GROUP * F, F), GROUP * F)
        return pltpu.make_async_remote_copy(
            src_ref=dqs.at[c], dst_ref=pg_out.at[0, :, cols], send_sem=dq_send.at[c], recv_sem=dq_recv.at[c],
            device_id=pipe_to, device_id_type=MESH,
        )

    SENDS_IN = {Z1: lev < LEVELS - 1, Z2: lev < LEVELS - 2, Z4: lev < LEVELS - 1}
    GETS_IN = {Z1: lev > 0, Z2: lev > 1, Z4: lev > 0}
    SENDS_OUT, GETS_OUT = GETS_IN, SENDS_IN

    def guarded(table, m, act):
        if m in table:
            pl.when(table[m])(act)
        else:
            act()

    def start_in(m, c):
        guarded(SENDS_IN, m, lambda: msg_in(m, c).start())

    def wait_in(m, c):
        guarded(GETS_IN, m, lambda: msg_in(m, c).wait_recv())

    def start_out(m, c):
        guarded(SENDS_OUT, m, lambda: msg_out(m, c).start())

    def wait_out(m, c):
        guarded(GETS_OUT, m, lambda: msg_out(m, c).wait_recv())

    def first_hop(c):
        for i in range(4):
            kv_load(c, i).wait()
        start_in(Z1, c)
        start_in(N, c)

        @pl.when(r == 0)
        def _():
            start_in(S1, c)

        start_in(Z2, c)

    def second_hop(c):
        wait_in(Z1, c)
        start_in(B2, c)

        @pl.when(r == 1)
        def _():
            start_in(S1, c)

        wait_in(Z2, c)
        start_in(S3, c)

    def third_hop(c):
        wait_in(B2, c)
        start_in(QO, c)
        start_in(Z4, c)
        wait_in(S1, c)
        wait_in(S3, c)
        start_in(PO, c)

    mask_load.wait()
    bias = []
    for d in range(4):
        flag = mask[0, blk, (blk + BLOCKS - 1 - d) % BLOCKS]
        bias.append(jnp.where((blk - 1 - d >= 0) & (flag == 1), jnp.float32(0.0), jnp.float32(-1e30)))

    def compute(c):
        wait_in(N, c)
        wait_in(QO, c)
        wait_in(Z4, c)
        wait_in(PO, c)
        for i in range(3):
            big_load(c, i).wait()

        def heads(ref):
            return jnp.concatenate([ref[c, :, h * F : (h + 1) * F] for h in range(GROUP)], axis=0)

        q = heads(qs)
        g = heads(gs)
        o = heads(os)

        def pairs(i):
            out = [noisy[c, :, i].reshape(2 * TOK, F)]
            for d in range(4):
                out.append(jnp.concatenate([win[c, 2 * d, i], win[c, 2 * d + 1, i]], axis=0))
            return out

        keys = pairs(0)
        values = pairs(1)
        prod = g.astype(F32) * o.astype(F32)
        high = prod.astype(BF)
        low = (prod - high.astype(F32)).astype(BF)
        ones = jnp.ones((16, F), BF)
        delta = (dot(ones, high, 1, 1) + dot(ones, low, 1, 1))[0:1]

        const = SCALE * LOG2E
        scores = [dot(k, q, 1, 1) for k in keys]
        tops = [s.max(axis=0, keepdims=True) * const for s in scores]
        top = tops[0]
        for d in range(4):
            top = jnp.maximum(top, tops[d + 1] + bias[d])
        exps = []
        total = jnp.zeros((1, ROWS), F32)
        for d, s in enumerate(scores):
            shift = top if d == 0 else top - bias[d - 1]
            e = jnp.exp2(s * const - shift)
            total = total + e.sum(axis=0, keepdims=True)
            exps.append(e)
        inv = 1.0 / total
        grads = {}
        for d in (1, 3, 4, 0, 2):
            p = exps[d] * inv
            dp = dot(values[d], g, 1, 1)
            ds = (p * (dp - delta)).astype(BF)
            grads[d] = ds
            dk = dot(ds, q, 1, 0) * SCALE
            dv = dot(p.astype(BF), g, 1, 0)
            if d == 0:
                own_n[c, 0] = dk[:TOK]
                own_n[c, 1] = dv[:TOK]
                part[c, 8, 0] = dk[TOK:].astype(BF)
                part[c, 8, 1] = dv[TOK:].astype(BF)
            else:
                s0 = 2 * (d - 1)
                part[c, s0, 0] = dk[:TOK].astype(BF)
                part[c, s0, 1] = dv[:TOK].astype(BF)
                part[c, s0 + 1, 0] = dk[TOK:].astype(BF)
                part[c, s0 + 1, 1] = dv[TOK:].astype(BF)
            if d == 3:
                start_out(PO, c)
                start_out(QO, c)
                pl.when(r == 0)(lambda: start_out(S1, c))
                pl.when(r == 1)(lambda: start_out(S3, c))
            elif d == 4:
                start_out(Z4, c)
                pl.when(r == 0)(lambda: start_out(Z2, c))
            elif d == 0:
                start_out(N, c)
        dq = sum(dot(keys[d], grads[d], 0, 0) for d in range(5))
        dq = (dq.T * SCALE).astype(BF)
        for h in range(GROUP):
            dqs[c, :, h * F : (h + 1) * F] = dq[h * TOK : (h + 1) * TOK]
        dq_copy(c).start()

    def wide(ref, *index):
        return ref[index].astype(F32)

    def second_out(c):
        for m in range(9):
            guarded(SENDS_IN, m, lambda: msg_in(m, c).wait_send())
        for m in (PO, QO, Z4):
            wait_out(m, c)
        part[c, 2 + other] = (wide(part, c, 2 + other) + wide(land, c, QO) + wide(land, c, Z4)).astype(BF)
        s = 2 * (2 - 2 * r) + other
        part[c, s] = (wide(part, c, s) + wide(land, c, PO)).astype(BF)
        pl.when(r == 0)(lambda: start_out(S3, c))
        pl.when(r == 1)(lambda: start_out(S1, c))
        start_out(B2, c)

    def third_out(c):
        for m in (S1, S3, B2):
            wait_out(m, c)
        first = wide(land, c, S1)
        third = wide(land, c, S3)
        part[c, 2 + par] = (
            wide(part, c, 2 + par) + wide(land, c, B2) + jnp.where(r == 1, first, third)
        ).astype(BF)
        start_out(Z1, c)

        @pl.when(r == 1)
        def _():
            part[c, 6 + par] = (wide(part, c, 6 + par) + third).astype(BF)
            start_out(Z2, c)

    def last_out(c):
        for m in (N, Z1, Z2):
            wait_out(m, c)
        cols = pl.ds(pl.multiple_of(c * F, F), F)
        clean = wide(land, c, Z1) + wide(land, c, Z2) + jnp.where(r == 0, wide(land, c, S1), 0.0)
        ck_out[0, :, cols] = clean[0].astype(BF)
        cv_out[0, :, cols] = clean[1].astype(BF)
        dirty = own_n[c] + wide(land, c, N)
        nk_out[0, :, cols] = dirty[0].astype(BF)
        nv_out[0, :, cols] = dirty[1].astype(BF)
        dq_copy(c).wait()
        for m in range(9):
            guarded(SENDS_OUT, m, lambda: msg_out(m, c).wait_send())

    pl.semaphore_wait(barrier, 8)
    for c in range(AHEAD):
        first_hop(c)
    lax.fori_loop(AHEAD, CHUNKS, load_kv, 0)
    lax.fori_loop(0, CHUNKS, load_big, 0)

    def stage(k, fn, lag, rate):
        for b in range(rate):
            c = rate * (k - lag) + b
            pl.when((c >= 0) & (c < CHUNKS))(functools.partial(fn, c))

    def step(k, _):
        pl.when(k + AHEAD < CHUNKS)(lambda: first_hop(k + AHEAD))
        stage(k, second_hop, 0, 1)
        stage(k, third_hop, 2, 1)
        stage(k, compute, 4, 1)
        stage(k, second_out, 6, 1)
        stage(k, third_out, 8, 1)
        stage(k, last_out, 10, 1)
        return 0

    lax.fori_loop(0, CHUNKS + 10, step, 0)


def finish(*refs):
    copies = [pltpu.make_async_copy(refs[i], refs[5 + i], refs[10].at[i]) for i in range(5)]
    for copy in copies:
        copy.start()
    for copy in copies:
        copy.wait()


def per_device(*args):
    noisy_q, noisy_k = args[:2]
    kv = jax.ShapeDtypeStruct(noisy_k.shape, BF)
    hbm = pl.BlockSpec(memory_space=pltpu.HBM)
    vmem = pl.BlockSpec(memory_space=pltpu.VMEM)
    dma = pltpu.SemaphoreType.DMA
    wide = (CHUNKS, TOK, GROUP * F)
    outs = pl.pallas_call(
        body,
        out_shape=(pltpu.VMEM(noisy_q.shape, BF),) + (pltpu.VMEM(noisy_k.shape, BF),) * 4,
        in_specs=[hbm] * 8,
        out_specs=(vmem,) * 5,
        scratch_shapes=[
            pltpu.SMEM((1, BLOCKS, BLOCKS), jnp.int32),
            dma(()),
            pltpu.VMEM(wide, BF),
            pltpu.VMEM(wide, BF),
            pltpu.VMEM(wide, BF),
            pltpu.VMEM((CHUNKS, 9, 2, TOK, F), BF),
            pltpu.VMEM((CHUNKS, 2, 2, TOK, F), BF),
            pltpu.VMEM((CHUNKS, 9, 2, TOK, F), BF),
            pltpu.VMEM((CHUNKS, 2, TOK, F), F32),
            pltpu.VMEM((CHUNKS, 9, 2, TOK, F), BF),
            pltpu.VMEM(wide, BF),
            dma((CHUNKS, 3)),
            dma((CHUNKS, 4)),
            dma((9, CHUNKS)),
            dma((9, CHUNKS)),
            dma((9, CHUNKS)),
            dma((9, CHUNKS)),
            dma((CHUNKS,)),
            dma((CHUNKS,)),
        ],
        compiler_params=pltpu.CompilerParams(
            collective_id=0, has_side_effects=True, vmem_limit_bytes=40 << 20
        ),
        cost_estimate=pl.CostEstimate(flops=3400000000, bytes_accessed=6 << 20, transcendentals=2700000),
    )(*[pltpu.with_memory_space_constraint(a, pltpu.HBM) for a in args])
    return pl.pallas_call(
        finish,
        out_shape=(jax.ShapeDtypeStruct(noisy_q.shape, BF), kv, kv, kv, kv),
        in_specs=[vmem] * 5,
        out_specs=(hbm,) * 5,
        scratch_shapes=[dma((5,))],
        compiler_params=pltpu.CompilerParams(vmem_limit_bytes=8 << 20),
    )(*outs)


def solution(mesh):
    three = P("pipe", "seq", None)
    return jax.shard_map(
        per_device, mesh=mesh, in_specs=(three,) * 7 + (P("pipe", None, None),), out_specs=(three,) * 5,
        check_vma=False,
    )
```
